256 devices in a mesh: row: 64 (over z, x, core), col: 4 (over y).
Axes of the slice: x: 4, y: 4, z: 8, core: 2. Of those that a mesh axis runs over, the one named last changes fastest.
Arguments:
- eigvecs: float32 [98304, 4096], P('row', 'col'), may hold values from -6 to 6
- reflectors: float32 [2, 98304, 128], P(None, 'row', 'col'), may hold values from -0.0546875 to 0.0546875
- factors: float32 [2, 128, 128], replicated, may hold values from -3 to 3
Outputs:
- transformed: float32 [98304, 4096], P('row', 'col')
The draws below stay inside these ranges and needn't reach their ends.
All inputs are finite; a program needn't handle non-finite values.
Results may differ from the reference program's by a relative error of at most 0.00012.
Values sent between devices are 32-bit elements; how exact they have to be, the bound alone decides.
A program may use at most 64 MiB of HBM per device.

```python
import jax
import jax.numpy as jnp
from jax import lax

M = 4096
NB = 128
BLOCKS = 2
N = 98304


def level_of(key, shape, cuts, low, high):
    def one(dim, blocks):
        steps = jax.random.uniform(jax.random.fold_in(jax.random.fold_in(key, 6), dim), (blocks,), jnp.float32, low / len(cuts), high / len(cuts))
        return jnp.repeat(jnp.exp(steps), shape[dim] // blocks).reshape((-1,) + (1,) * (len(shape) - dim - 1))

    level = one(*cuts[0])
    for cut in cuts[1:]:
        level = level * one(*cut)
    return level


def bell_draw(stream_key, shape, deviation, reach, shards=(), dtype=jnp.bfloat16):
    result = jax.random.normal(stream_key, shape, jnp.float32) * deviation
    if len(shards) > 0:
        result = level_of(stream_key, shape, shards, -0.22, 0.18) * result
    return jnp.clip(result, min=-reach, max=reach).astype(dtype)


def setup_inputs(seed: int = 0) -> dict:
    splits = jax.random.split(jax.random.key(seed), 4)
    return {
        "eigvecs": bell_draw(splits[0], (N, M), 1.0, 6.0, ((0, 64), (1, 4)), jnp.float32),
        "reflectors": bell_draw(splits[1], (BLOCKS, N, NB), (N // 9) ** -0.5, 0.0546875, ((1, 64), (2, 4)), jnp.float32),
        "factors": bell_draw(splits[2], (BLOCKS, NB, NB), 0.5, 3.0, (), jnp.float32),
    }


def product(left, right):
    return jnp.dot(left, right, precision=lax.Precision.HIGHEST, preferred_element_type=jnp.float32)


def reference(eigvecs, reflectors, factors):
    vectors = eigvecs
    for index_block in range(BLOCKS):
        householder = reflectors[index_block]
        triangle = jnp.triu(factors[index_block])
        inner = product(householder.T, vectors)
        coefficient = product(triangle, inner)
        vectors = vectors - product(householder, coefficient)
    return vectors
```

```python
import jax
import jax.numpy as jnp
from jax import lax
from jax.experimental import pallas as pl
from jax.experimental.pallas import tpu as pltpu
from jax.sharding import PartitionSpec as P

MESH = pl.DeviceIdType.MESH
F32, BF16 = jnp.float32, jnp.bfloat16
BLOCKS = 2
X_SIZE, Z_SIZE, Y_SIZE = 4, 8, 4
SETS = 4
CHUNKS = 6

SET_GROUPS = (((0, 0), (0, 1)), ((3, 0), (1, 1)), ((3, 1), (1, 0)), ((2, 0), (2, 1)))


def split(value):
    high = value.astype(BF16)
    return high, (value - high.astype(F32)).astype(BF16)


def dot(left, right, dims):
    return lax.dot_general(left, right, (dims, ((), ())), preferred_element_type=F32)


def product(left, right, dims=((1,), (0,))):
    (lh, ll), (rh, rl) = left, right
    return dot(lh, rh, dims) + (dot(lh, rl, dims) + dot(ll, rh, dims))


def reduce_kernel(
    x_hbm, v_hbm, f_ref, v_out, ch_out, cl_out,
    x_buf, xh, xl, v_all, s_loc, core_in, x_in, x_sum, z_in, s_sum,
    g_loc, g_core, g_xin, g_xsum, g_zin, g_sum,
    x_sem, v_sem, vo_sem, vs_sem, vr_sem,
    c_s, c_r, xs_s, xs_r, zs_s, zs_r, zg_s, zg_r, xg_s, xg_r, cg_s, cg_r,
):
    row, y = lax.axis_index("row"), lax.axis_index("col")
    z, x, core = row // 8, (row // 2) % 4, row % 2
    rows = x_hbm.shape[0] // CHUNKS

    def at(z_, x_, core_, y_):
        return ((z_ * 4 + x_) * 2 + core_, y_)

    other = at(z, x, 1 - core, y)
    x_peer = [at(z, (x + d) % 4, core, y) for d in range(1, 4)]
    z_peer = [at((z + d) % 8, x, core, y) for d in range(1, 8)]
    up, down = at(z, x, core, (y + 1) % 4), at(z, x, core, (y + 3) % 4)
    half = pl.multiple_of(core * 512, 512)
    other_half = pl.multiple_of((1 - core) * 512, 512)

    x_copies = []
    for i in range(CHUNKS):
        part = pl.ds(i * rows, rows)
        copy = pltpu.make_async_copy(x_hbm.at[part], x_buf.at[part], x_sem.at[i])
        copy.start()
        x_copies.append(copy)
    own = pltpu.make_async_copy(v_hbm, v_all.at[0], v_sem)
    own.start()

    barrier = pltpu.get_barrier_semaphore()
    for device in [up, down, other] + x_peer + z_peer:
        pl.semaphore_signal(barrier, inc=1, device_id=device, device_id_type=MESH)
    pl.semaphore_wait(barrier, 13)

    pending = []

    def send(src, dst, s_sem, r_sem, device):
        copy = pltpu.make_async_remote_copy(
            src_ref=src, dst_ref=dst, send_sem=s_sem, recv_sem=r_sem, device_id=device, device_id_type=MESH
        )
        copy.start()
        pending.append(copy)
        return copy

    from_down, from_up, opposite = [None, None], [None, None], [None, None]
    for i in range(2):
        from_down[i] = send(v_hbm.at[i], v_all.at[3, i], vs_sem.at[0, i], vr_sem.at[0, i], up)
        b = 1 - i
        from_up[b] = send(v_hbm.at[b], v_all.at[1, b], vs_sem.at[1, b], vr_sem.at[1, b], down)

    for i in range(CHUNKS):
        x_copies[i].wait()

    @pl.loop(0, CHUNKS)
    def _(i):
        part = pl.ds(pl.multiple_of(i * rows, rows), rows)
        high, low = split(x_buf[part, :])
        xh[part, :] = high
        xl[part, :] = low

    own.wait()

    copies = [{} for _ in range(SETS)]

    def p0(i):
        groups = SET_GROUPS[i]
        vh, vl = split(jnp.concatenate([v_all[r, b] for r, b in groups], axis=0))
        both = jnp.concatenate([vh, vl], axis=0)

        @pl.loop(0, 4)
        def _(j):
            cols = pl.ds(pl.multiple_of(j * 256, 256), 256)
            first = dot(both, xh[:, cols], ((1,), (0,)))
            second = dot(vh, xl[:, cols], ((1,), (0,)))
            s_loc[i, :, cols] = first[:64] + (first[64:] + second)

        copies[i]["c"] = send(
            s_loc.at[i, :, pl.ds(other_half, 512)], core_in.at[i], c_s.at[i], c_r.at[i], other
        )

    def p1(i):
        copies[i]["c"].wait_recv()
        mine = pl.ds(half, 512)
        s_loc[i, :, mine] = s_loc[i, :, mine] + core_in[i]
        copies[i]["x"] = [
            send(
                s_loc.at[i, pl.ds(pl.multiple_of((x + d) % 4 * 16, 16), 16), mine],
                x_in.at[i, d - 1], xs_s.at[i, d - 1], xs_r.at[i, d - 1], x_peer[d - 1],
            )
            for d in range(1, 4)
        ]

    def z_tile(z_):
        return pl.ds(pl.multiple_of(z_ // 4 * 8, 8), 8), pl.ds(pl.multiple_of(z_ % 4 * 128, 128), 128)

    def p2(i):
        for copy in copies[i]["x"]:
            copy.wait_recv()
        mine = s_loc[i, pl.ds(pl.multiple_of(x * 16, 16), 16), pl.ds(half, 512)]
        x_sum[i] = (mine + x_in[i, 0]) + (x_in[i, 1] + x_in[i, 2])
        copies[i]["z"] = []
        for d in range(1, 8):
            tile_rows, tile_cols = z_tile((z + d) % 8)
            copies[i]["z"].append(
                send(
                    x_sum.at[i, tile_rows, tile_cols], z_in.at[i, d - 1],
                    zs_s.at[i, d - 1], zs_r.at[i, d - 1], z_peer[d - 1],
                )
            )

    def groups_of(i):
        return SET_GROUPS[i]

    def group_at(i):
        (r0, b0), (r1, b1) = groups_of(i)
        g = x // 2
        return r0 + g * (r1 - r0), b0 + g * (b1 - b0)

    x_row = x % 2 * 16

    def p3(i):
        for copy in copies[i]["z"]:
            copy.wait_recv()
        tile_rows, tile_cols = z_tile(z)
        total = x_sum[i, tile_rows, tile_cols]
        for d in range(7):
            total = total + z_in[i, d]
        r, b = group_at(i)
        spot = s_sum.at[
            r, b,
            pl.ds(pl.multiple_of(x_row + z // 4 * 8, 8), 8),
            pl.ds(pl.multiple_of(half + z % 4 * 128, 128), 128),
        ]
        spot[...] = total
        copies[i]["zg"] = [
            send(spot, spot, zg_s.at[i, d - 1], zg_r.at[i, d - 1], z_peer[d - 1]) for d in range(1, 8)
        ]

    def p4(i):
        for copy in copies[i]["zg"]:
            copy.wait_recv()
        r, b = group_at(i)
        spot = s_sum.at[r, b, pl.ds(pl.multiple_of(x_row, 16), 16), pl.ds(half, 512)]
        copies[i]["xg"] = [
            send(spot, spot, xg_s.at[i, d - 1], xg_r.at[i, d - 1], x_peer[d - 1]) for d in range(1, 4)
        ]

    def p5(i):
        for copy in copies[i]["xg"]:
            copy.wait_recv()
        copies[i]["cg"] = []
        for k, (r, b) in enumerate(groups_of(i)):
            spot = s_sum.at[r, b, :, pl.ds(half, 512)]
            copies[i]["cg"].append(send(spot, spot, cg_s.at[i, k], cg_r.at[i, k], other))

    def p6(i):
        for copy in copies[i]["cg"]:
            copy.wait_recv()

    def slot(a):
        return (a + Y_SIZE - y) % Y_SIZE

    def g0():
        ordered = [split(jnp.concatenate([v_all[slot(a), b] for a in range(4)], axis=0)) for b in range(2)]
        g_loc[...] = product(ordered[1], ordered[0], ((1,), (1,)))
        spot = g_loc.at[pl.ds(pl.multiple_of((1 - core) * 64, 64), 64)]
        gc["c"] = send(spot, g_core, c_s.at[SETS], c_r.at[SETS], other)

    gc = {}

    def g1():
        gc["c"].wait_recv()
        mine = pl.ds(pl.multiple_of(core * 64, 64), 64)
        g_loc[mine, :] = g_loc[mine, :] + g_core[...]
        gc["x"] = [
            send(
                g_loc.at[pl.ds(pl.multiple_of(core * 64 + (x + d) % 4 * 16, 16), 16)],
                g_xin.at[d - 1], xs_s.at[SETS, d - 1], xs_r.at[SETS, d - 1], x_peer[d - 1],
            )
            for d in range(1, 4)
        ]

    def g2():
        for copy in gc["x"]:
            copy.wait_recv()
        mine = g_loc[pl.ds(pl.multiple_of(core * 64 + x * 16, 16), 16), :]
        g_xsum[...] = (mine + g_xin[0]) + (g_xin[1] + g_xin[2])
        g_zin[z] = g_xsum[...]
        gc["z"] = [
            send(g_xsum, g_zin.at[z], zs_s.at[SETS, d - 1], zs_r.at[SETS, d - 1], z_peer[d - 1])
            for d in range(1, 8)
        ]

    def g3():
        for copy in gc["z"]:
            copy.wait_recv()
        total = g_zin[0]
        for d in range(1, 8):
            total = total + g_zin[d]
        spot = g_sum.at[pl.ds(pl.multiple_of(core * 64 + x * 16, 16), 16)]
        spot[...] = total
        gc["xg"] = [
            send(spot, spot, xg_s.at[SETS, d - 1], xg_r.at[SETS, d - 1], x_peer[d - 1]) for d in range(1, 4)
        ]

    def g4():
        for copy in gc["xg"]:
            copy.wait_recv()
        spot = g_sum.at[pl.ds(pl.multiple_of(core * 64, 64), 64)]
        gc["cg"] = send(spot, spot, cg_s.at[SETS, 0], cg_r.at[SETS, 0], other)

    def g5():
        gc["cg"].wait_recv()

    v_copies = []

    def keep(r, b):
        copy = pltpu.make_async_copy(v_all.at[r, b], v_out.at[r, b], vo_sem.at[r, b])
        copy.start()
        v_copies.append(copy)

    keep(0, 0)
    keep(0, 1)
    p0(0)
    from_down[0].wait_recv()
    opposite[0] = send(v_all.at[3, 0], v_all.at[2, 0], vs_sem.at[2, 0], vr_sem.at[2, 0], up)
    from_up[1].wait_recv()
    opposite[1] = send(v_all.at[1, 1], v_all.at[2, 1], vs_sem.at[2, 1], vr_sem.at[2, 1], down)
    keep(3, 0)
    keep(1, 1)
    p1(0)
    p0(1)
    p2(0)
    p1(1)
    p3(0)
    p2(1)
    p4(0)
    p3(1)
    from_down[1].wait_recv()
    from_up[0].wait_recv()
    keep(3, 1)
    keep(1, 0)
    p0(2)
    p5(0)
    p4(1)
    p1(2)
    p5(1)
    p2(2)
    p3(2)
    opposite[0].wait_recv()
    opposite[1].wait_recv()
    p0(3)
    keep(2, 0)
    keep(2, 1)
    g0()
    p4(2)
    p1(3)
    g1()
    p5(2)
    p2(3)
    g2()
    p3(3)
    g3()
    p4(3)
    g4()
    p5(3)
    g5()
    p6(0)
    p6(1)
    p6(2)
    p6(3)

    upper = lax.broadcasted_iota(jnp.int32, (128, 128), 0) <= lax.broadcasted_iota(jnp.int32, (128, 128), 1)
    t0, t1 = (split(jnp.where(upper, f_ref[b], 0.0)) for b in range(2))
    g = split(g_sum[...])

    for j in range(4):
        cols = pl.ds(j * 256, 256)
        s0, s1 = (jnp.concatenate([s_sum[slot(a), b, :, cols] for a in range(4)], axis=0) for b in range(2))
        c0 = product(t0, split(s0))
        c0 = split(c0)
        c1 = split(product(t1, split(s1 - product(g, c0))))
        for b, (high, low) in enumerate((c0, c1)):
            for a in range(4):
                ch_out[slot(a), b, :, cols] = high[a * 32 : (a + 1) * 32]
                cl_out[slot(a), b, :, cols] = low[a * 32 : (a + 1) * 32]

    for copy in v_copies:
        copy.wait()
    for copy in pending:
        copy.wait_send()


def update_kernel(x_ref, v_ref, ch_ref, cl_ref, out_ref):
    vh, vl = split(v_ref[...])
    dims = ((0,), (0,))
    ch = ch_ref[...]
    out_ref[...] = x_ref[...] - (dot(vh, ch, dims) + (dot(vh, cl_ref[...], dims) + dot(vl, ch, dims)))


def body(eigvecs, reflectors, factors):
    rows, columns = eigvecs.shape
    own = reflectors.transpose(0, 2, 1)
    group = own.shape[1]
    dma = pltpu.SemaphoreType.DMA
    any_space = pl.BlockSpec(memory_space=pl.ANY)
    hbm = pl.BlockSpec(memory_space=pltpu.HBM)
    vmem = pl.BlockSpec(memory_space=pltpu.VMEM)
    v_all, ch, cl = pl.pallas_call(
        reduce_kernel,
        out_shape=[
            jax.ShapeDtypeStruct((Y_SIZE, BLOCKS, group, rows), F32),
            jax.ShapeDtypeStruct((Y_SIZE, BLOCKS, group, columns), BF16),
            jax.ShapeDtypeStruct((Y_SIZE, BLOCKS, group, columns), BF16),
        ],
        in_specs=[hbm, hbm, vmem],
        out_specs=[any_space, vmem, vmem],
        scratch_shapes=[
            pltpu.VMEM((rows, columns), F32),
            pltpu.VMEM((rows, columns), BF16),
            pltpu.VMEM((rows, columns), BF16),
            pltpu.VMEM((Y_SIZE, BLOCKS, group, rows), F32),
            pltpu.VMEM((SETS, 64, columns), F32),
            pltpu.VMEM((SETS, 64, 512), F32),
            pltpu.VMEM((SETS, 3, 16, 512), F32),
            pltpu.VMEM((SETS, 16, 512), F32),
            pltpu.VMEM((SETS, 7, 8, 128), F32),
            pltpu.VMEM((Y_SIZE, BLOCKS, group, columns), F32),
            pltpu.VMEM((128, 128), F32),
            pltpu.VMEM((64, 128), F32),
            pltpu.VMEM((3, 16, 128), F32),
            pltpu.VMEM((16, 128), F32),
            pltpu.VMEM((8, 16, 128), F32),
            pltpu.VMEM((128, 128), F32),
            dma((CHUNKS,)), dma, dma((Y_SIZE, BLOCKS)), dma((3, 2)), dma((3, 2)),
            dma((SETS + 1,)), dma((SETS + 1,)),
            dma((SETS + 1, 3)), dma((SETS + 1, 3)),
            dma((SETS + 1, 7)), dma((SETS + 1, 7)),
            dma((SETS, 7)), dma((SETS, 7)),
            dma((SETS + 1, 3)), dma((SETS + 1, 3)),
            dma((SETS + 1, 2)), dma((SETS + 1, 2)),
        ],
        compiler_params=pltpu.CompilerParams(
            collective_id=0, has_side_effects=True, vmem_limit_bytes=40 * 2**20
        ),
        name="gather_and_reduce",
    )(eigvecs, own, factors)

    depth = Y_SIZE * BLOCKS * group
    step = 256
    return pl.pallas_call(
        update_kernel,
        grid=(rows // step,),
        out_shape=jax.ShapeDtypeStruct((rows, columns), F32),
        in_specs=[
            pl.BlockSpec((step, columns), lambda i: (i, 0)),
            pl.BlockSpec((depth, step), lambda i: (0, i)),
            pl.BlockSpec((depth, columns), lambda i: (0, 0)),
            pl.BlockSpec((depth, columns), lambda i: (0, 0)),
        ],
        out_specs=pl.BlockSpec((step, columns), lambda i: (i, 0)),
        compiler_params=pltpu.CompilerParams(vmem_limit_bytes=32 * 2**20),
        name="update",
    )(eigvecs, v_all.reshape(depth, rows), ch.reshape(depth, columns), cl.reshape(depth, columns))


def solution(mesh):
    placed = (P("row", "col"), P(None, "row", "col"), P())
    return jax.shard_map(
        body, mesh=mesh, in_specs=placed, out_specs=P("row", "col"), check_vma=False
    )
```

```python
import jax
import jax.numpy as jnp
from jax import lax
from jax.experimental import pallas as pl
from jax.experimental.pallas import tpu as pltpu
from jax.sharding import PartitionSpec as P

MESH = pl.DeviceIdType.MESH
F32, BF16 = jnp.float32, jnp.bfloat16
BLOCKS = 2
Y_SIZE = 4
CHUNKS = 6

SET_GROUPS = ((0, 1, 3, 6), (7, 2), (4, 5))
PARTS = ((0, (0, 1)), (0, (3, 6)), (1, (7, 2)), (2, (4, 5)))
SETS = len(SET_GROUPS)


def split(value):
    high = value.astype(BF16)
    return high, (value - high.astype(F32)).astype(BF16)


def dot(left, right, dims):
    return lax.dot_general(left, right, (dims, ((), ())), preferred_element_type=F32)


def product(left, right, dims=((1,), (0,))):
    (lh, ll), (rh, rl) = left, right
    return dot(lh, rh, dims) + (dot(lh, rl, dims) + dot(ll, rh, dims))


def reduce_kernel(
    x_hbm, v_hbm, f_hbm, v_out, ch_out, cl_out,
    x_buf, xh, xl, v_all, f_ref, s_loc, core_in, x_in, x_sum, z_in, z_full, s_sum,
    g_loc, g_core, g_xin, g_zin, g_sum,
    x_sem, v_sem, vo_sem, vs_sem, vr_sem,
    c_s, c_r, xs_s, xs_r, zs_s, zs_r, zg_s, zg_r, xg_s, xg_r, cg_s, cg_r,
):
    row, y = lax.axis_index("row"), lax.axis_index("col")
    z, x, core = row // 8, (row // 2) % 4, row % 2
    rows = x_hbm.shape[0] // CHUNKS

    def at(z_, x_, core_, y_):
        return ((z_ * 4 + x_) * 2 + core_, y_)

    other = at(z, x, 1 - core, y)
    x_peer = [at(z, (x + d) % 4, core, y) for d in range(1, 4)]
    z_peer = [at((z + d) % 8, x, core, y) for d in range(1, 8)]
    up, down = at(z, x, core, (y + 1) % 4), at(z, x, core, (y + 3) % 4)
    mine = pl.ds(pl.multiple_of(core * 512, 512), 512)
    theirs = pl.ds(pl.multiple_of((1 - core) * 512, 512), 512)

    barrier = pltpu.get_barrier_semaphore()
    for device in [up, down, other] + x_peer + z_peer:
        pl.semaphore_signal(barrier, inc=1, device_id=device, device_id_type=MESH)

    x_copies = []
    for i in range(CHUNKS):
        part = pl.ds(i * rows, rows)
        copy = pltpu.make_async_copy(x_hbm.at[part], x_buf.at[part], x_sem.at[i])
        copy.start()
        x_copies.append(copy)
    own = pltpu.make_async_copy(v_hbm, v_all.at[0:2], v_sem.at[0])
    own.start()
    factors = pltpu.make_async_copy(f_hbm, f_ref, v_sem.at[1])
    factors.start()

    def take(i):
        x_copies[i].wait()

        @pl.loop(0, rows // 64)
        def _(j):
            part = pl.ds(pl.multiple_of(i * rows + j * 64, 64), 64)
            high, low = split(x_buf[part, :])
            xh[part, :] = high
            xl[part, :] = low

    for i in range(CHUNKS // 2):
        take(i)

    pl.semaphore_wait(barrier, 13)

    pending = []

    def send(src, dst, s_sem, r_sem, device):
        copy = pltpu.make_async_remote_copy(
            src_ref=src, dst_ref=dst, send_sem=s_sem, recv_sem=r_sem, device_id=device, device_id_type=MESH
        )
        copy.start()
        pending.append(copy)
        return copy

    from_down, from_up, opposite = [None, None], [None, None], [None, None]
    for i in range(2):
        from_down[i] = send(v_hbm.at[i], v_all.at[6 + i], vs_sem.at[0, i], vr_sem.at[0, i], up)
        b = 1 - i
        from_up[b] = send(v_hbm.at[b], v_all.at[2 + b], vs_sem.at[1, b], vr_sem.at[1, b], down)

    for i in range(CHUNKS // 2, CHUNKS):
        take(i)

    own.wait()

    core_copies, x_sends, z_sends, z_shares, x_shares, core_shares = ([[] for _ in range(SETS + 1)] for _ in range(6))
    kept = []

    def arrived(copies):
        for copy in copies:
            copy.wait_recv()

    def partial(k):
        i, groups = PARTS[k]
        base = 32 * SET_GROUPS[i].index(groups[0])
        vh, vl = split(jnp.concatenate([v_all[g] for g in groups], axis=0))
        both = jnp.concatenate([vh, vl], axis=0)

        @pl.loop(0, 4)
        def _(j):
            cols = pl.ds(pl.multiple_of(j * 256, 256), 256)
            first = dot(both, xh[:, cols], ((1,), (0,)))
            second = dot(vh, xl[:, cols], ((1,), (0,)))
            s_loc[i][base : base + 64, cols] = first[:64] + (first[64:] + second)

        here = pl.ds(base, 64)
        core_copies[i].append(send(s_loc[i].at[here, theirs], core_in[i].at[here], c_s.at[k], c_r.at[k], other))
        for g in groups:
            copy = pltpu.make_async_copy(v_all.at[g], v_out.at[g], vo_sem.at[g])
            copy.start()
            kept.append(copy)

    def span(i):
        return 8 * len(SET_GROUPS[i])

    def x_rows(i, x_):
        return pl.ds(pl.multiple_of(x_ * span(i), 16), span(i))

    def to_x(i):
        arrived(core_copies[i])
        s_loc[i][:, mine] = s_loc[i][:, mine] + core_in[i][...]
        for d in range(1, 4):
            x_sends[i].append(
                send(
                    s_loc[i].at[x_rows(i, (x + d) % 4), mine], x_in[i].at[d - 1],
                    xs_s.at[i, d - 1], xs_r.at[i, d - 1], x_peer[d - 1],
                )
            )

    def z_tile(i, z_):
        n = 8 // (span(i) // 8)
        width = 512 // n
        return pl.multiple_of(z_ // n * 8, 8), pl.multiple_of(z_ % n * width, 128), width

    def x_total(i):
        arrived(x_sends[i])
        return (s_loc[i][x_rows(i, x), mine] + x_in[i][0]) + (x_in[i][1] + x_in[i][2])

    def to_z(i):
        x_sum[i][...] = x_total(i)
        for d in range(1, 8):
            r, c, width = z_tile(i, (z + d) % 8)
            z_sends[i].append(
                send(
                    x_sum[i].at[pl.ds(r, 8), pl.ds(c, width)], z_in[i].at[d - 1],
                    zs_s.at[i, d - 1], zs_r.at[i, d - 1], z_peer[d - 1],
                )
            )

    def to_z_whole(i):
        z_full[z] = x_total(i)
        for d in range(1, 8):
            z_sends[i].append(
                send(z_full.at[z], z_full.at[z], zs_s.at[i, d - 1], zs_r.at[i, d - 1], z_peer[d - 1])
            )

    def place(i):
        if i == 0:
            return x * (x + 1) // 2, 0
        g, first = x // 2, pl.multiple_of(x % 2 * 16, 16)
        return (7 - 5 * g if i == 1 else 4 + g), first

    def share_z(i):
        arrived(z_sends[i])
        r, c, width = z_tile(i, z)
        total = x_sum[i][pl.ds(r, 8), pl.ds(c, width)]
        for d in range(7):
            total = total + z_in[i][d]
        g, first = place(i)
        spot = s_sum.at[
            g, pl.ds(pl.multiple_of(first + r, 8), 8), pl.ds(pl.multiple_of(core * 512 + c, 128), width)
        ]
        spot[...] = total
        for d in range(1, 8):
            z_shares[i].append(send(spot, spot, zg_s.at[i, d - 1], zg_r.at[i, d - 1], z_peer[d - 1]))

    def share_x(i, whole=False):
        g, first = place(i)
        spot = s_sum.at[g, pl.ds(first, span(i)), mine]
        if whole:
            arrived(z_sends[i])
            total = z_full[0]
            for d in range(1, 8):
                total = total + z_full[d]
            spot[...] = total
        else:
            arrived(z_shares[i])
        for d in range(1, 4):
            x_shares[i].append(send(spot, spot, xg_s.at[i, d - 1], xg_r.at[i, d - 1], x_peer[d - 1]))

    def share_core(i):
        arrived(x_shares[i])
        for k, g in enumerate(SET_GROUPS[i]):
            spot = s_sum.at[g, :, mine]
            core_shares[i].append(send(spot, spot, cg_s.at[i, k], cg_r.at[i, k], other))

    def slot(a):
        return (a + Y_SIZE - y) % Y_SIZE

    g_rows = pl.ds(pl.multiple_of(core * 64, 64), 64)
    g_spot = pl.ds(pl.multiple_of(core * 64 + x * 16, 16), 16)

    def g_partial():
        ordered = [split(jnp.concatenate([v_all[2 * slot(a) + b] for a in range(4)], axis=0)) for b in range(2)]
        g_loc[...] = product(ordered[1], ordered[0], ((1,), (1,)))
        spot = g_loc.at[pl.ds(pl.multiple_of((1 - core) * 64, 64), 64)]
        core_copies[SETS].append(send(spot, g_core, c_s.at[4], c_r.at[4], other))

    def g_to_x():
        arrived(core_copies[SETS])
        g_loc[g_rows, :] = g_loc[g_rows, :] + g_core[...]
        for d in range(1, 4):
            spot = g_loc.at[pl.ds(pl.multiple_of(core * 64 + (x + d) % 4 * 16, 16), 16)]
            x_sends[SETS].append(
                send(spot, g_xin.at[d - 1], xs_s.at[SETS, d - 1], xs_r.at[SETS, d - 1], x_peer[d - 1])
            )

    def g_to_z():
        arrived(x_sends[SETS])
        g_zin[z] = (g_loc[g_spot, :] + g_xin[0]) + (g_xin[1] + g_xin[2])
        for d in range(1, 8):
            z_sends[SETS].append(
                send(g_zin.at[z], g_zin.at[z], zs_s.at[SETS, d - 1], zs_r.at[SETS, d - 1], z_peer[d - 1])
            )

    def g_share_x():
        arrived(z_sends[SETS])
        total = g_zin[0]
        for d in range(1, 8):
            total = total + g_zin[d]
        spot = g_sum.at[g_spot]
        spot[...] = total
        for d in range(1, 4):
            x_shares[SETS].append(send(spot, spot, xg_s.at[SETS, d - 1], xg_r.at[SETS, d - 1], x_peer[d - 1]))

    def g_share_core():
        arrived(x_shares[SETS])
        spot = g_sum.at[g_rows]
        core_shares[SETS].append(send(spot, spot, cg_s.at[SETS, 0], cg_r.at[SETS, 0], other))

    partial(0)
    from_down[0].wait_recv()
    opposite[0] = send(v_all.at[6], v_all.at[4], vs_sem.at[2, 0], vr_sem.at[2, 0], up)
    from_up[1].wait_recv()
    opposite[1] = send(v_all.at[3], v_all.at[5], vs_sem.at[2, 1], vr_sem.at[2, 1], down)
    partial(1)
    to_x(0)
    from_down[1].wait_recv()
    from_up[0].wait_recv()
    partial(2)
    to_z(0)
    to_x(1)
    opposite[0].wait_recv()
    opposite[1].wait_recv()
    partial(3)
    g_partial()
    to_z(1)
    to_x(2)
    g_to_x()
    share_z(0)
    to_z_whole(2)
    g_to_z()
    share_z(1)
    share_x(0)
    share_x(1)
    share_core(0)
    g_share_x()
    share_x(2, whole=True)
    share_core(1)
    g_share_core()
    share_core(2)

    factors.wait()
    upper = lax.broadcasted_iota(jnp.int32, (128, 128), 0) <= lax.broadcasted_iota(jnp.int32, (128, 128), 1)
    t0, t1 = (split(jnp.where(upper, f_ref[b], 0.0)) for b in range(2))
    for i in (0, 1, SETS, 2):
        arrived(core_shares[i])
    g = split(g_sum[...])

    for j in range(4):
        cols = pl.ds(j * 256, 256)
        s0, s1 = (jnp.concatenate([s_sum[2 * slot(a) + b, :, cols] for a in range(4)], axis=0) for b in range(2))
        c0 = split(product(t0, split(s0)))
        c1 = split(product(t1, split(s1 - product(g, c0))))
        for b, (high, low) in enumerate((c0, c1)):
            for a in range(4):
                ch_out[2 * slot(a) + b, :, cols] = high[a * 32 : (a + 1) * 32]
                cl_out[2 * slot(a) + b, :, cols] = low[a * 32 : (a + 1) * 32]

    for copy in kept:
        copy.wait()
    for copy in pending:
        copy.wait_send()


def update_kernel(x_ref, v_ref, ch_ref, cl_ref, out_ref):
    vh, vl = split(v_ref[...])
    dims = ((0,), (0,))
    ch = ch_ref[...]
    out_ref[...] = x_ref[...] - (dot(vh, ch, dims) + (dot(vh, cl_ref[...], dims) + dot(vl, ch, dims)))


def body(eigvecs, reflectors, factors):
    rows, columns = eigvecs.shape
    own = reflectors.transpose(0, 2, 1)
    group = own.shape[1]
    dma = pltpu.SemaphoreType.DMA
    any_space = pl.BlockSpec(memory_space=pl.ANY)
    vmem = pl.BlockSpec(memory_space=pltpu.VMEM)
    groups = Y_SIZE * BLOCKS
    heights = [group * len(groups_) for groups_ in SET_GROUPS]
    v_all, ch, cl = pl.pallas_call(
        reduce_kernel,
        out_shape=[
            jax.ShapeDtypeStruct((groups, group, rows), F32),
            jax.ShapeDtypeStruct((groups, group, columns), BF16),
            jax.ShapeDtypeStruct((groups, group, columns), BF16),
        ],
        in_specs=[any_space, any_space, any_space],
        out_specs=[any_space, vmem, vmem],
        scratch_shapes=[
            pltpu.VMEM((rows, columns), F32),
            pltpu.VMEM((rows, columns), BF16),
            pltpu.VMEM((rows, columns), BF16),
            pltpu.VMEM((groups, group, rows), F32),
            pltpu.VMEM(factors.shape, F32),
            [pltpu.VMEM((h, columns), F32) for h in heights],
            [pltpu.VMEM((h, 512), F32) for h in heights],
            [pltpu.VMEM((3, h // 4, 512), F32) for h in heights],
            [pltpu.VMEM((h // 4, 512), F32) for h in heights],
            [pltpu.VMEM((7, 8, 2 * h), F32) for h in heights],
            pltpu.VMEM((8, 16, 512), F32),
            pltpu.VMEM((groups, group, columns), F32),
            pltpu.VMEM((128, 128), F32),
            pltpu.VMEM((64, 128), F32),
            pltpu.VMEM((3, 16, 128), F32),
            pltpu.VMEM((8, 16, 128), F32),
            pltpu.VMEM((128, 128), F32),
            dma((CHUNKS,)), dma((2,)), dma((groups,)), dma((3, 2)), dma((3, 2)),
            dma((5,)), dma((5,)),
            dma((SETS + 1, 3)), dma((SETS + 1, 3)),
            dma((SETS + 1, 7)), dma((SETS + 1, 7)),
            dma((SETS, 7)), dma((SETS, 7)),
            dma((SETS + 1, 3)), dma((SETS + 1, 3)),
            dma((SETS + 1, 4)), dma((SETS + 1, 4)),
        ],
        compiler_params=pltpu.CompilerParams(
            collective_id=0, has_side_effects=True, vmem_limit_bytes=40 * 2**20
        ),
        name="gather_and_reduce",
    )(*(pltpu.with_memory_space_constraint(operand, pltpu.HBM) for operand in (eigvecs, own, factors)))

    depth = groups * group
    step = 256
    return pl.pallas_call(
        update_kernel,
        grid=(rows // step,),
        out_shape=jax.ShapeDtypeStruct((rows, columns), F32),
        in_specs=[
            pl.BlockSpec((step, columns), lambda i: (i, 0)),
            pl.BlockSpec((depth, step), lambda i: (0, i)),
            pl.BlockSpec((depth, columns), lambda i: (0, 0)),
            pl.BlockSpec((depth, columns), lambda i: (0, 0)),
        ],
        out_specs=pl.BlockSpec((step, columns), lambda i: (i, 0)),
        compiler_params=pltpu.CompilerParams(vmem_limit_bytes=32 * 2**20),
        name="update",
    )(eigvecs, v_all.reshape(depth, rows), ch.reshape(depth, columns), cl.reshape(depth, columns))


def solution(mesh):
    placed = (P("row", "col"), P(None, "row", "col"), P())
    return jax.shard_map(
        body, mesh=mesh, in_specs=placed, out_specs=P("row", "col"), check_vma=False
    )
```

```python
import jax
import jax.numpy as jnp
from jax import lax
from jax.experimental import pallas as pl
from jax.experimental.pallas import tpu as pltpu
from jax.sharding import PartitionSpec as P

MESH = pl.DeviceIdType.MESH
F32, BF16 = jnp.float32, jnp.bfloat16
BLOCKS = 2
Y_SIZE = 4
CHUNKS = 6

SET_GROUPS = ((0, 1), (6, 3), (7, 2), (4, 5))
SETS = len(SET_GROUPS)
STEPS = sorted(
    ((dz, dx) for dz in range(8) for dx in range(4) if dz or dx),
    key=lambda step: -min(step[0], 8 - step[0]) - min(step[1], 4 - step[1]),
)


def line(g):
    return g % 2 * 128 + g // 2 * 32


def split(value):
    high = value.astype(BF16)
    return high, (value - high.astype(F32)).astype(BF16)


def dot(left, right, dims):
    return lax.dot_general(left, right, (dims, ((), ())), preferred_element_type=F32)


def product(left, right, dims=((1,), (0,))):
    (lh, ll), (rh, rl) = left, right
    return dot(lh, rh, dims) + (dot(lh, rl, dims) + dot(ll, rh, dims))


def reduce_kernel(
    x_hbm, v_hbm, f_hbm, vh_out, vl_out, ch_out, cl_out,
    x_buf, xh, xl, v_all, vh_all, vl_all, vh_t, vl_t, f_ref, tri, s_loc, core_in, x_in, x_sum, z_in, d_in, s_sum, ch, cl,
    g_loc, g_core, g_xin, g_zin, g_sum,
    x_sem, v_sem, out_sem, vs_sem, vr_sem,
    c_s, c_r, xs_s, xs_r, zs_s, zs_r, zg_s, zg_r, xg_s, xg_r, cg_s, cg_r, ds_s, ds_r, dg_s, dg_r, entered,
):
    row, y = lax.axis_index("row"), lax.axis_index("col")
    z, x, core = row // 8, (row // 2) % 4, row % 2
    rows = x_hbm.shape[0] // CHUNKS

    def at(z_, x_, core_, y_):
        return ((z_ * 4 + x_) * 2 + core_, y_)

    other = at(z, x, 1 - core, y)
    x_peer = [at(z, (x + d) % 4, core, y) for d in range(1, 4)]
    z_peer = [at((z + d) % 8, x, core, y) for d in range(1, 8)]
    plane = [at((z + dz) % 8, (x + dx) % 4, core, y) for dz, dx in STEPS]
    y_peer = [at(z, x, core, (y + d) % 4) for d in range(1, 4)]
    up, down = y_peer[0], y_peer[2]
    mine = pl.ds(pl.multiple_of(core * 512, 512), 512)
    theirs = pl.ds(pl.multiple_of((1 - core) * 512, 512), 512)

    barrier = pltpu.get_barrier_semaphore()
    for device in y_peer + [other] + x_peer + z_peer:
        pl.semaphore_signal(barrier, inc=1, device_id=device, device_id_type=MESH)

    x_copies = []
    for i in range(CHUNKS):
        part = pl.ds(i * rows, rows)
        copy = pltpu.make_async_copy(x_hbm.at[part], x_buf.at[part], x_sem.at[i])
        copy.start()
        x_copies.append(copy)
    own = pltpu.make_async_copy(v_hbm, v_all.at[0:2], v_sem.at[0])
    own.start()
    factors = pltpu.make_async_copy(f_hbm, f_ref, v_sem.at[1])
    factors.start()

    def take(i):
        x_copies[i].wait()

        @pl.loop(0, rows // 64)
        def _(j):
            part = pl.ds(pl.multiple_of(i * rows + j * 64, 64), 64)
            high, low = split(x_buf[part, :])
            xh[part, :] = high
            xl[part, :] = low

    for i in range(CHUNKS // 2):
        take(i)

    pl.semaphore_wait(barrier, 14)

    pending = []

    def send(src, dst, s_sem, r_sem, device):
        copy = pltpu.make_async_remote_copy(
            src_ref=src, dst_ref=dst, send_sem=s_sem, recv_sem=r_sem, device_id=device, device_id_type=MESH
        )
        copy.start()
        pending.append(copy)
        return copy

    from_down, from_up, opposite = [None, None], [None, None], [None, None]
    for i in range(2):
        from_down[i] = send(v_hbm.at[i], v_all.at[6 + i], vs_sem.at[0, i], vr_sem.at[0, i], up)
        b = 1 - i
        from_up[b] = send(v_hbm.at[b], v_all.at[2 + b], vs_sem.at[1, b], vr_sem.at[1, b], down)

    for device in z_peer:
        pl.semaphore_signal(entered, inc=1, device_id=device, device_id_type=MESH)

    for i in range(CHUNKS // 2, CHUNKS):
        take(i)

    own.wait()

    core_copies, x_sends, z_sends, z_shares, x_shares, core_shares = ([[] for _ in range(SETS + 1)] for _ in range(6))

    def arrived(copies):
        while copies:
            copies.pop(0).wait_recv()

    def flush():
        while pending:
            pending.pop(0).wait_send()

    def partial(i):
        groups = SET_GROUPS[i]
        vh, vl = split(jnp.concatenate([v_all[g] for g in groups], axis=0))
        both = jnp.concatenate([vh, vl], axis=0)

        def columns(part):
            first = dot(both, xh[:, part], ((1,), (0,)))
            second = dot(vh, xl[:, part], ((1,), (0,)))
            s_loc[i, :, part] = first[:64] + (first[64:] + second)

        columns(theirs)
        core_copies[i].append(send(s_loc.at[i, :, theirs], core_in.at[i], c_s.at[i], c_r.at[i], other))
        columns(mine)
        for n, g in enumerate(groups):
            spot = slice(line(g), line(g) + 32)
            vh_all[spot] = vh[32 * n : 32 * n + 32]
            vl_all[spot] = vl[32 * n : 32 * n + 32]

    def add_core(i):
        arrived(core_copies[i])
        s_loc[i, :, mine] = s_loc[i, :, mine] + core_in[i]

    def group(i, half):
        first, second = SET_GROUPS[i]
        return first + half * (second - first)

    def x_rows(x_):
        return pl.ds(pl.multiple_of(x_ * 16, 16), 16)

    def z_tile(z_):
        return pl.ds(pl.multiple_of(z_ // 4 * 8, 8), 8), pl.multiple_of(z_ % 4 * 128, 128)

    def to_x(i):
        add_core(i)
        for d in range(1, 4):
            x_sends[i].append(
                send(
                    s_loc.at[i, x_rows((x + d) % 4), mine], x_in.at[i, d - 1],
                    xs_s.at[i, d - 1], xs_r.at[i, d - 1], x_peer[d - 1],
                )
            )

    def to_z(i):
        arrived(x_sends[i])
        x_sum[i] = (s_loc[i, x_rows(x), mine] + x_in[i, 0]) + (x_in[i, 1] + x_in[i, 2])
        for d in range(1, 8):
            r, c = z_tile((z + d) % 8)
            z_sends[i].append(
                send(
                    x_sum.at[i, r, pl.ds(c, 128)], z_in.at[i, d - 1],
                    zs_s.at[i, d - 1], zs_r.at[i, d - 1], z_peer[d - 1],
                )
            )

    def share_z(i):
        arrived(z_sends[i])
        r, c = z_tile(z)
        total = x_sum[i, r, pl.ds(c, 128)]
        for d in range(7):
            total = total + z_in[i, d]
        first = pl.multiple_of(x % 2 * 16 + z // 4 * 8, 8)
        spot = s_sum.at[group(i, x // 2), pl.ds(first, 8), pl.ds(pl.multiple_of(core * 512 + c, 128), 128)]
        spot[...] = total
        for d in range(1, 8):
            z_shares[i].append(send(spot, spot, zg_s.at[i, d - 1], zg_r.at[i, d - 1], z_peer[d - 1]))

    def share_x(i):
        arrived(z_shares[i])
        spot = s_sum.at[group(i, x // 2), pl.ds(pl.multiple_of(x % 2 * 16, 16), 16), mine]
        for d in range(1, 4):
            x_shares[i].append(send(spot, spot, xg_s.at[i, d - 1], xg_r.at[i, d - 1], x_peer[d - 1]))

    def tile(z_, x_):
        return pl.ds(pl.multiple_of(z_ * 8, 8), 8), pl.ds(pl.multiple_of(core * 512 + x_ * 128, 128), 128)

    def to_plane(i):
        add_core(i)
        for k, (dz, dx) in enumerate(STEPS):
            r, c = tile((z + dz) % 8, (x + dx) % 4)
            x_sends[i].append(
                send(s_loc.at[i, r, c], d_in.at[k], ds_s.at[k], ds_r.at[k], plane[k])
            )

    def share_plane(i):
        arrived(x_sends[i])
        r, c = tile(z, x)
        total = s_loc[i, r, c]
        for k in range(len(STEPS)):
            total = total + d_in[k]
        spot = s_sum.at[group(i, z // 4), pl.ds(pl.multiple_of(z % 4 * 8, 8), 8), c]
        spot[...] = total
        for k in range(len(STEPS)):
            x_shares[i].append(send(spot, spot, dg_s.at[k], dg_r.at[k], plane[k]))

    def share_core(i):
        arrived(x_shares[i])
        for k, g in enumerate(SET_GROUPS[i]):
            spot = s_sum.at[g, :, mine]
            core_shares[i].append(send(spot, spot, cg_s.at[i, k], cg_r.at[i, k], other))

    PAIRS = ((0, 0), (0, 3), (1, 3), (3, 0))
    g_half = pl.ds(pl.multiple_of(core * 16, 16), 16)
    g_other = pl.ds(pl.multiple_of((1 - core) * 16, 16), 16)

    def g_partial():
        second, first = (
            tuple(jnp.concatenate([v[line(g) : line(g) + 32] for g in groups], axis=0) for v in (vh_all, vl_all))
            for groups in ((1, 3, 7), (0, 6))
        )
        pairs = product(second, first, ((1,), (1,)))
        place = {0: 0, 1: 1, 3: 2}, {0: 0, 3: 1}
        g_loc[...] = jnp.concatenate(
            [
                pairs[32 * place[0][i] : 32 * place[0][i] + 32, 32 * place[1][j] : 32 * place[1][j] + 32]
                for i, j in PAIRS
            ],
            axis=1,
        )
        core_copies[SETS].append(send(g_loc.at[g_other], g_core, c_s.at[SETS], c_r.at[SETS], other))

    def g_to_x():
        arrived(core_copies[SETS])
        g_xin[x] = g_loc[g_half, :] + g_core[...]
        for d in range(1, 4):
            x_sends[SETS].append(
                send(g_xin.at[x], g_xin.at[x], xs_s.at[SETS, d - 1], xs_r.at[SETS, d - 1], x_peer[d - 1])
            )

    def g_to_z():
        arrived(x_sends[SETS])
        g_zin[z] = (g_xin[0] + g_xin[1]) + (g_xin[2] + g_xin[3])
        for d in range(1, 8):
            z_sends[SETS].append(
                send(g_zin.at[z], g_zin.at[z], zs_s.at[SETS, d - 1], zs_r.at[SETS, d - 1], z_peer[d - 1])
            )

    def g_share_core():
        arrived(z_sends[SETS])
        total = g_zin[0]
        for d in range(1, 8):
            total = total + g_zin[d]
        spot = g_sum.at[0, g_half]
        spot[...] = total
        core_shares[SETS].append(send(spot, spot, cg_s.at[SETS, 0], cg_r.at[SETS, 0], other))

    def g_share_y():
        arrived(core_shares[SETS])
        for d in range(1, 4):
            x_shares[SETS].append(
                send(g_sum.at[0], g_sum.at[4 - d], xg_s.at[SETS, d - 1], xg_r.at[SETS, d - 1], y_peer[d - 1])
            )

    def g_whole():
        arrived(x_shares[SETS])
        lines = []
        for i in range(4):
            blocks = []
            for j in range(4):
                d = (i - j) % 4
                source = (i, i, i + 3, i + 1)[d] % 4
                blocks.append(g_sum[source, :, 32 * d : 32 * d + 32])
            lines.append(jnp.concatenate(blocks, axis=1))
        return jnp.concatenate(lines, axis=0)

    outs = []

    def leave(src, dst):
        copy = pltpu.make_async_copy(src, dst, out_sem.at[len(outs)])
        copy.start()
        outs.append(copy)

    partial(0)
    to_x(0)

    factors.wait()
    upper = lax.broadcasted_iota(jnp.int32, (128, 128), 0) <= lax.broadcasted_iota(jnp.int32, (128, 128), 1)
    turn = (Y_SIZE - y) % Y_SIZE * 32
    for b in range(2):
        tri[b] = pltpu.roll(pltpu.roll(jnp.where(upper, f_ref[b], 0.0), turn, 0), turn, 1)

    from_down[0].wait_recv()
    opposite[0] = send(v_all.at[6], v_all.at[4], vs_sem.at[2, 0], vr_sem.at[2, 0], up)
    from_up[1].wait_recv()
    opposite[1] = send(v_all.at[3], v_all.at[5], vs_sem.at[2, 1], vr_sem.at[2, 1], down)
    partial(1)
    to_z(0)
    to_x(1)
    from_down[1].wait_recv()
    from_up[0].wait_recv()
    partial(2)
    g_partial()
    to_x(2)
    share_z(0)
    to_z(1)
    g_to_x()
    pl.semaphore_wait(entered, 7)
    opposite[0].wait_recv()
    opposite[1].wait_recv()
    partial(3)
    to_plane(3)
    to_z(2)
    g_to_z()
    share_x(0)
    share_z(1)

    @pl.loop(0, CHUNKS)
    def _(i):
        part = pl.ds(pl.multiple_of(i * rows, rows), rows)
        vh_t[part, :] = vh_all[:, part].T
        vl_t[part, :] = vl_all[:, part].T

    leave(vh_t, vh_out)
    leave(vl_t, vl_out)

    share_core(0)
    share_z(2)
    g_share_core()
    share_x(1)
    g_share_y()
    share_plane(3)
    share_x(2)
    share_core(1)
    share_core(2)
    for i in range(3):
        arrived(core_shares[i])

    t0, t1 = split(tri[0]), split(tri[1])
    mixed = product(split(product(t1, split(g_whole()))), t0)
    matrix = split(
        jnp.concatenate(
            [
                jnp.concatenate([tri[0], jnp.zeros((128, 128), F32)], axis=1),
                jnp.concatenate([-mixed, tri[1]], axis=1),
            ],
            axis=0,
        )
    )
    flush()
    share_core(3)
    arrived(core_shares[3])
    for j in range(4):
        cols = pl.ds(j * 256, 256)
        sums = jnp.concatenate([s_sum[n, :, cols] for n in (0, 2, 4, 6, 1, 3, 5, 7)], axis=0)
        ch[:, cols], cl[:, cols] = split(product(matrix, split(sums)))
        leave(ch.at[:, cols], ch_out.at[:, cols])
        leave(cl.at[:, cols], cl_out.at[:, cols])

    for copy in outs:
        copy.wait()
    flush()


def update_kernel(x_ref, vh_ref, vl_ref, ch_ref, cl_ref, out, buffer, sem):
    step = x_ref.shape[0] // CHUNKS
    copies = []
    for i in range(CHUNKS):
        part = pl.ds(i * step, step)
        for j in range(4):
            cols = pl.ds(j * 256, 256)
            change = product((vh_ref[part, :], vl_ref[part, :]), (ch_ref[:, cols], cl_ref[:, cols]))
            buffer[part, cols] = x_ref[part, cols] - change
        copy = pltpu.make_async_copy(buffer.at[part], out.at[part], sem.at[i])
        copy.start()
        copies.append(copy)
    for copy in copies:
        copy.wait()


def body(eigvecs, reflectors, factors):
    rows, columns = eigvecs.shape
    own = reflectors.transpose(0, 2, 1)
    group = own.shape[1]
    dma = pltpu.SemaphoreType.DMA
    any_space = pl.BlockSpec(memory_space=pl.ANY)
    groups = Y_SIZE * BLOCKS
    depth = groups * group
    vh, vl, ch, cl = pl.pallas_call(
        reduce_kernel,
        out_shape=[
            jax.ShapeDtypeStruct((rows, depth), BF16),
            jax.ShapeDtypeStruct((rows, depth), BF16),
            jax.ShapeDtypeStruct((depth, columns), BF16),
            jax.ShapeDtypeStruct((depth, columns), BF16),
        ],
        in_specs=[any_space, any_space, any_space],
        out_specs=[any_space, any_space, any_space, any_space],
        scratch_shapes=[
            pltpu.VMEM((rows, columns), F32),
            pltpu.VMEM((rows, columns), BF16),
            pltpu.VMEM((rows, columns), BF16),
            pltpu.VMEM((groups, group, rows), F32),
            pltpu.VMEM((depth, rows), BF16),
            pltpu.VMEM((depth, rows), BF16),
            pltpu.VMEM((rows, depth), BF16),
            pltpu.VMEM((rows, depth), BF16),
            pltpu.VMEM(factors.shape, F32),
            pltpu.VMEM(factors.shape, F32),
            pltpu.VMEM((SETS, 64, columns), F32),
            pltpu.VMEM((SETS, 64, 512), F32),
            pltpu.VMEM((SETS - 1, 3, 16, 512), F32),
            pltpu.VMEM((SETS - 1, 16, 512), F32),
            pltpu.VMEM((SETS - 1, 7, 8, 128), F32),
            pltpu.VMEM((len(STEPS), 8, 128), F32),
            pltpu.VMEM((groups, group, columns), F32),
            pltpu.VMEM((depth, columns), BF16),
            pltpu.VMEM((depth, columns), BF16),
            pltpu.VMEM((32, 128), F32),
            pltpu.VMEM((16, 128), F32),
            pltpu.VMEM((4, 16, 128), F32),
            pltpu.VMEM((8, 16, 128), F32),
            pltpu.VMEM((4, 32, 128), F32),
            dma((CHUNKS,)), dma((2,)), dma((10,)), dma((3, 2)), dma((3, 2)),
            dma((SETS + 1,)), dma((SETS + 1,)),
            dma((SETS + 1, 3)), dma((SETS + 1, 3)),
            dma((SETS + 1, 7)), dma((SETS + 1, 7)),
            dma((SETS, 7)), dma((SETS, 7)),
            dma((SETS + 1, 3)), dma((SETS + 1, 3)),
            dma((SETS + 1, 2)), dma((SETS + 1, 2)),
            dma((len(STEPS),)), dma((len(STEPS),)),
            dma((len(STEPS),)), dma((len(STEPS),)),
            pltpu.SemaphoreType.REGULAR,
        ],
        compiler_params=pltpu.CompilerParams(
            collective_id=0, has_side_effects=True, vmem_limit_bytes=40 * 2**20
        ),
        name="gather_and_reduce",
    )(*(pltpu.with_memory_space_constraint(operand, pltpu.HBM) for operand in (eigvecs, own, factors)))

    operands = (eigvecs, vh, vl, ch, cl)
    return pl.pallas_call(
        update_kernel,
        out_shape=jax.ShapeDtypeStruct((rows, columns), F32),
        in_specs=[pl.BlockSpec(memory_space=pltpu.VMEM)] * len(operands),
        out_specs=any_space,
        scratch_shapes=[pltpu.VMEM((rows, columns), F32), dma((CHUNKS,))],
        compiler_params=pltpu.CompilerParams(vmem_limit_bytes=16 * 2**20),
        name="update",
    )(*(pltpu.with_memory_space_constraint(operand, pltpu.VMEM) for operand in operands))


def solution(mesh):
    placed = (P("row", "col"), P(None, "row", "col"), P())
    return jax.shard_map(
        body, mesh=mesh, in_specs=placed, out_specs=P("row", "col"), check_vma=False
    )
```

```python
import jax
import jax.numpy as jnp
from jax import lax
from jax.experimental import pallas as pl
from jax.experimental.pallas import tpu as pltpu
from jax.sharding import PartitionSpec as P

MESH = pl.DeviceIdType.MESH
F32, BF16 = jnp.float32, jnp.bfloat16
BLOCKS = 2
Y_SIZE = 4
CHUNKS = 6
PIECES = 12

SET_GROUPS = ((0, 1), (6, 3), (7, 2), (4, 5))
SETS = len(SET_GROUPS)
STEPS = sorted(
    ((dz, dx) for dz in range(8) for dx in range(4) if dz or dx),
    key=lambda step: -min(step[0], 8 - step[0]) - min(step[1], 4 - step[1]),
)


def line(g):
    return g % 2 * 128 + g // 2 * 32


def split(value):
    high = value.astype(BF16)
    return high, (value - high.astype(F32)).astype(BF16)


def dot(left, right, dims):
    return lax.dot_general(left, right, (dims, ((), ())), preferred_element_type=F32)


def product(left, right, dims=((1,), (0,))):
    (lh, ll), (rh, rl) = left, right
    return dot(lh, rh, dims) + (dot(lh, rl, dims) + dot(ll, rh, dims))


def reduce_kernel(
    x_hbm, v_hbm, f_hbm, vh_out, vl_out, ch_out, cl_out,
    x_buf, xh, xl, v_all, vh_all, vl_all, vh_t, vl_t, f_ref, tri, s_loc, core_in, x_in, x_sum, z_in, d_in, s_sum, c_part, ch, cl,
    g_loc, g_core, g_xin, g_zin, g_sum,
    x_sem, v_sem, out_sem, vs_sem, vr_sem,
    c_s, c_r, xs_s, xs_r, zs_s, zs_r, zg_s, zg_r, xg_s, xg_r, cg_s, cg_r, ds_s, ds_r, dg_s, dg_r, greeted,
):
    row, y = lax.axis_index("row"), lax.axis_index("col")
    z, x, core = row // 8, (row // 2) % 4, row % 2
    rows = x_hbm.shape[0] // CHUNKS

    def at(z_, x_, core_, y_):
        return ((z_ * 4 + x_) * 2 + core_, y_)

    other = at(z, x, 1 - core, y)
    x_peer = [at(z, (x + d) % 4, core, y) for d in range(1, 4)]
    z_peer = [at((z + d) % 8, x, core, y) for d in range(1, 8)]
    plane = [at((z + dz) % 8, (x + dx) % 4, core, y) for dz, dx in STEPS]
    y_peer = [at(z, x, core, (y + d) % 4) for d in range(1, 4)]
    up, down = y_peer[0], y_peer[2]
    mine = pl.ds(pl.multiple_of(core * 512, 512), 512)
    theirs = pl.ds(pl.multiple_of((1 - core) * 512, 512), 512)

    z_near = [at((z + d) % 8, x, core, y) for d in (1, 7)]
    z_next = [at((z + d) % 8, x, core, y) for d in (2, 6)]
    x_near = [x_peer[0], x_peer[2]]

    def greet(semaphore, devices):
        for device in devices:
            pl.semaphore_signal(semaphore, inc=1, device_id=device, device_id_type=MESH)

    barrier = pltpu.get_barrier_semaphore()
    greet(barrier, [up, down, other] + x_near + z_near)

    own = pltpu.make_async_copy(v_hbm, v_all.at[0:2], v_sem.at[0])
    own.start()
    factors = pltpu.make_async_copy(f_hbm, f_ref, v_sem.at[1])
    factors.start()

    def take(i):
        x_copies[i].wait()

        @pl.loop(0, rows // 64)
        def _(j):
            part = pl.ds(pl.multiple_of(i * rows + j * 64, 64), 64)
            high, low = split(x_buf[part, :])
            xh[part, :] = high
            xl[part, :] = low

    own.wait()
    pl.semaphore_wait(barrier, 7)
    pending = []

    def send(src, dst, s_sem, r_sem, device):
        copy = pltpu.make_async_remote_copy(
            src_ref=src, dst_ref=dst, send_sem=s_sem, recv_sem=r_sem, device_id=device, device_id_type=MESH
        )
        copy.start()
        pending.append(copy)
        return copy

    from_down, from_up, opposite = [None, None], [None, None], [None, None]
    for i in range(2):
        from_down[i] = send(v_all.at[i], v_all.at[6 + i], vs_sem.at[0, i], vr_sem.at[0, i], up)
        b = 1 - i
        from_up[b] = send(v_all.at[b], v_all.at[2 + b], vs_sem.at[1, b], vr_sem.at[1, b], down)

    x_copies = []
    for i in range(CHUNKS):
        part = pl.ds(i * rows, rows)
        copy = pltpu.make_async_copy(x_hbm.at[part], x_buf.at[part], x_sem.at[i])
        copy.start()
        x_copies.append(copy)
    greet(greeted.at[0], z_near)
    greet(greeted.at[1], x_near)
    for i in range(CHUNKS):
        take(i)
        if i == 2:
            pl.semaphore_wait(greeted.at[0], 2)
            greet(greeted.at[2], z_next)

    core_copies, x_sends, z_sends, z_shares, x_shares, core_shares = ([[] for _ in range(SETS + 1)] for _ in range(6))

    def arrived(copies):
        while copies:
            copies.pop(0).wait_recv()

    def flush(left=0):
        while len(pending) > left:
            pending.pop(0).wait_send()

    def partial(i):
        groups = SET_GROUPS[i]
        vh, vl = split(jnp.concatenate([v_all[g] for g in groups], axis=0))
        both = jnp.concatenate([vh, vl], axis=0)

        def columns(part):
            first = dot(both, xh[:, part], ((1,), (0,)))
            second = dot(vh, xl[:, part], ((1,), (0,)))
            s_loc[i, :, part] = first[:64] + (first[64:] + second)

        columns(theirs)
        core_copies[i].append(send(s_loc.at[i, :, theirs], core_in.at[i], c_s.at[i], c_r.at[i], other))
        columns(mine)
        for n, g in enumerate(groups):
            spot = slice(line(g), line(g) + 32)
            vh_all[spot] = vh[32 * n : 32 * n + 32]
            vl_all[spot] = vl[32 * n : 32 * n + 32]

    def add_core(i):
        arrived(core_copies[i])
        s_loc[i, :, mine] = s_loc[i, :, mine] + core_in[i]

    def group(i, half):
        first, second = SET_GROUPS[i]
        return first + half * (second - first)

    def x_rows(x_):
        return pl.ds(pl.multiple_of(x_ * 16, 16), 16)

    def z_tile(z_):
        return pl.ds(pl.multiple_of(z_ // 4 * 8, 8), 8), pl.multiple_of(z_ % 4 * 128, 128)

    def to_x(i):
        add_core(i)
        for d in range(1, 4):
            x_sends[i].append(
                send(
                    s_loc.at[i, x_rows((x + d) % 4), mine], x_in.at[i, d - 1],
                    xs_s.at[i, d - 1], xs_r.at[i, d - 1], x_peer[d - 1],
                )
            )

    def to_z(i):
        arrived(x_sends[i])
        x_sum[i] = (s_loc[i, x_rows(x), mine] + x_in[i, 0]) + (x_in[i, 1] + x_in[i, 2])
        for d in range(1, 8):
            r, c = z_tile((z + d) % 8)
            z_sends[i].append(
                send(
                    x_sum.at[i, r, pl.ds(c, 128)], z_in.at[i, d - 1],
                    zs_s.at[i, d - 1], zs_r.at[i, d - 1], z_peer[d - 1],
                )
            )

    def share_z(i):
        arrived(z_sends[i])
        r, c = z_tile(z)
        total = x_sum[i, r, pl.ds(c, 128)]
        for d in range(7):
            total = total + z_in[i, d]
        first = pl.multiple_of(x % 2 * 16 + z // 4 * 8, 8)
        spot = s_sum.at[group(i, x // 2), pl.ds(first, 8), pl.ds(pl.multiple_of(core * 512 + c, 128), 128)]
        spot[...] = total
        for d in range(1, 8):
            z_shares[i].append(send(spot, spot, zg_s.at[i, d - 1], zg_r.at[i, d - 1], z_peer[d - 1]))

    def share_x(i):
        arrived(z_shares[i])
        spot = s_sum.at[group(i, x // 2), pl.ds(pl.multiple_of(x % 2 * 16, 16), 16), mine]
        for d in range(1, 4):
            x_shares[i].append(send(spot, spot, xg_s.at[i, d - 1], xg_r.at[i, d - 1], x_peer[d - 1]))

    def tile(z_, x_):
        return pl.ds(pl.multiple_of(z_ * 8, 8), 8), pl.ds(pl.multiple_of(core * 512 + x_ * 128, 128), 128)

    def to_plane(i):
        add_core(i)
        for k, (dz, dx) in enumerate(STEPS):
            r, c = tile((z + dz) % 8, (x + dx) % 4)
            x_sends[i].append(
                send(s_loc.at[i, r, c], d_in.at[i - 2, k], ds_s.at[i - 2, k], ds_r.at[i - 2, k], plane[k])
            )

    def share_plane(i):
        arrived(x_sends[i])
        r, c = tile(z, x)
        total = s_loc[i, r, c]
        for k in range(len(STEPS)):
            total = total + d_in[i - 2, k]
        spot = s_sum.at[group(i, z // 4), pl.ds(pl.multiple_of(z % 4 * 8, 8), 8), c]
        spot[...] = total
        for k in range(len(STEPS)):
            x_shares[i].append(send(spot, spot, dg_s.at[i - 2, k], dg_r.at[i - 2, k], plane[k]))

    def share_core(i):
        arrived(x_shares[i])
        for k, g in enumerate(SET_GROUPS[i]):
            spot = s_sum.at[g, :, mine]
            core_shares[i].append(send(spot, spot, cg_s.at[i, k], cg_r.at[i, k], other))

    PAIRS = ((0, 0), (0, 3), (1, 3), (3, 0))
    g_half = pl.ds(pl.multiple_of(core * 16, 16), 16)
    g_other = pl.ds(pl.multiple_of((1 - core) * 16, 16), 16)

    def g_partial():
        second, first = (
            tuple(jnp.concatenate([v[line(g) : line(g) + 32] for g in groups], axis=0) for v in (vh_all, vl_all))
            for groups in ((1, 3, 7), (0, 6))
        )
        pairs = product(second, first, ((1,), (1,)))
        place = {0: 0, 1: 1, 3: 2}, {0: 0, 3: 1}
        g_loc[...] = jnp.concatenate(
            [
                pairs[32 * place[0][i] : 32 * place[0][i] + 32, 32 * place[1][j] : 32 * place[1][j] + 32]
                for i, j in PAIRS
            ],
            axis=1,
        )
        core_copies[SETS].append(send(g_loc.at[g_other], g_core, c_s.at[SETS], c_r.at[SETS], other))

    def g_to_x():
        arrived(core_copies[SETS])
        g_xin[x] = g_loc[g_half, :] + g_core[...]
        for d in range(1, 4):
            x_sends[SETS].append(
                send(g_xin.at[x], g_xin.at[x], xs_s.at[SETS, d - 1], xs_r.at[SETS, d - 1], x_peer[d - 1])
            )

    def g_to_z():
        arrived(x_sends[SETS])
        g_zin[z] = (g_xin[0] + g_xin[1]) + (g_xin[2] + g_xin[3])
        for d in range(1, 8):
            z_sends[SETS].append(
                send(g_zin.at[z], g_zin.at[z], zs_s.at[SETS, d - 1], zs_r.at[SETS, d - 1], z_peer[d - 1])
            )

    def g_share_core():
        arrived(z_sends[SETS])
        total = g_zin[0]
        for d in range(1, 8):
            total = total + g_zin[d]
        spot = g_sum.at[0, g_half]
        spot[...] = total
        core_shares[SETS].append(send(spot, spot, cg_s.at[SETS, 0], cg_r.at[SETS, 0], other))

    def g_share_y():
        arrived(core_shares[SETS])
        for d in range(1, 4):
            x_shares[SETS].append(
                send(g_sum.at[0], g_sum.at[4 - d], xg_s.at[SETS, d - 1], xg_r.at[SETS, d - 1], y_peer[d - 1])
            )

    def g_whole():
        arrived(x_shares[SETS])
        lines = []
        for i in range(4):
            blocks = []
            for j in range(4):
                d = (i - j) % 4
                source = (i, i, i + 3, i + 1)[d] % 4
                blocks.append(g_sum[source, :, 32 * d : 32 * d + 32])
            lines.append(jnp.concatenate(blocks, axis=1))
        return jnp.concatenate(lines, axis=0)

    outs = []

    def leave(src, dst):
        copy = pltpu.make_async_copy(src, dst, out_sem.at[len(outs)])
        copy.start()
        outs.append(copy)

    partial(0)
    pl.semaphore_wait(greeted.at[1], 2)
    to_x(0)
    pl.semaphore_wait(greeted.at[2], 2)
    greet(greeted.at[3], z_peer)

    from_down[0].wait_recv()
    opposite[0] = send(v_all.at[6], v_all.at[4], vs_sem.at[2, 0], vr_sem.at[2, 0], up)
    from_up[1].wait_recv()
    opposite[1] = send(v_all.at[3], v_all.at[5], vs_sem.at[2, 1], vr_sem.at[2, 1], down)
    partial(1)
    to_x(1)

    factors.wait()
    upper = lax.broadcasted_iota(jnp.int32, (128, 128), 0) <= lax.broadcasted_iota(jnp.int32, (128, 128), 1)
    turn = (Y_SIZE - y) % Y_SIZE * 32
    for b in range(2):
        tri[b] = pltpu.roll(pltpu.roll(jnp.where(upper, f_ref[b], 0.0), turn, 0), turn, 1)

    from_down[1].wait_recv()
    from_up[0].wait_recv()
    partial(2)
    to_z(0)
    g_partial()
    pl.semaphore_wait(greeted.at[3], 7)
    to_plane(2)
    g_to_x()
    to_z(1)
    opposite[0].wait_recv()
    opposite[1].wait_recv()
    partial(3)
    to_plane(3)
    share_z(0)
    g_to_z()
    share_z(1)
    share_plane(2)
    share_x(0)

    @pl.loop(0, CHUNKS)
    def _(i):
        part = pl.ds(pl.multiple_of(i * rows, rows), rows)
        vh_t[part, :] = vh_all[:, part].T
        vl_t[part, :] = vl_all[:, part].T

    flush(40)
    leave(vh_t, vh_out)
    leave(vl_t, vl_out)

    share_plane(3)
    g_share_core()
    share_x(1)
    g_share_y()
    share_core(0)
    share_core(2)

    t0, t1 = split(tri[0]), split(tri[1])
    mixed = product(split(product(t1, split(g_whole()))), t0)
    matrix = split(
        jnp.concatenate(
            [
                jnp.concatenate([tri[0], jnp.zeros((128, 128), F32)], axis=1),
                jnp.concatenate([-mixed, tri[1]], axis=1),
            ],
            axis=0,
        )
    )

    def part_of(i):
        high, low = matrix
        return jnp.concatenate([m[:, line(g) : line(g) + 32] for m in (high, high, low) for g in SET_GROUPS[i]], axis=1)

    def term(i, wide, cols):
        sh, sl = split(jnp.concatenate([s_sum[g, :, cols] for g in SET_GROUPS[i]], axis=0))
        return dot(wide, jnp.concatenate([sh, sl, sh], axis=0), ((1,), (0,)))

    def add_set(i, first=False):
        arrived(core_shares[i])
        wide = part_of(i)
        for j in range(4):
            cols = pl.ds(j * 256, 256)
            c_part[:, cols] = term(i, wide, cols) if first else c_part[:, cols] + term(i, wide, cols)

    def finish(start, wide):
        for j in range(2):
            cols = pl.ds(pl.multiple_of(start + j * 256, 256), 256)
            ch[:, cols], cl[:, cols] = split(c_part[:, cols] + term(3, wide, cols))
            leave(ch.at[:, cols], ch_out.at[:, cols])
            leave(cl.at[:, cols], cl_out.at[:, cols])

    add_set(0, first=True)
    share_core(1)
    flush(40)
    add_set(2)
    share_core(3)
    add_set(1)
    wide = part_of(3)
    finish(core * 512, wide)
    arrived(core_shares[3])
    finish((1 - core) * 512, wide)

    for copy in outs:
        copy.wait()
    flush()


def update_kernel(x_ref, vh_ref, vl_ref, ch_ref, cl_ref, out, buffer, sem):
    step = x_ref.shape[0] // PIECES
    copies = []
    for i in range(PIECES):
        part = pl.ds(i * step, step)
        for j in range(4):
            cols = pl.ds(j * 256, 256)
            change = product((vh_ref[part, :], vl_ref[part, :]), (ch_ref[:, cols], cl_ref[:, cols]))
            buffer[part, cols] = x_ref[part, cols] - change
        copy = pltpu.make_async_copy(buffer.at[part], out.at[part], sem.at[i])
        copy.start()
        copies.append(copy)
    for copy in copies:
        copy.wait()


def body(eigvecs, reflectors, factors):
    rows, columns = eigvecs.shape
    own = reflectors.transpose(0, 2, 1)
    group = own.shape[1]
    dma = pltpu.SemaphoreType.DMA
    any_space = pl.BlockSpec(memory_space=pl.ANY)
    groups = Y_SIZE * BLOCKS
    depth = groups * group
    vh, vl, ch, cl = pl.pallas_call(
        reduce_kernel,
        out_shape=[
            jax.ShapeDtypeStruct((rows, depth), BF16),
            jax.ShapeDtypeStruct((rows, depth), BF16),
            jax.ShapeDtypeStruct((depth, columns), BF16),
            jax.ShapeDtypeStruct((depth, columns), BF16),
        ],
        in_specs=[any_space, any_space, any_space],
        out_specs=[any_space, any_space, any_space, any_space],
        scratch_shapes=[
            pltpu.VMEM((rows, columns), F32),
            pltpu.VMEM((rows, columns), BF16),
            pltpu.VMEM((rows, columns), BF16),
            pltpu.VMEM((groups, group, rows), F32),
            pltpu.VMEM((depth, rows), BF16),
            pltpu.VMEM((depth, rows), BF16),
            pltpu.VMEM((rows, depth), BF16),
            pltpu.VMEM((rows, depth), BF16),
            pltpu.VMEM(factors.shape, F32),
            pltpu.VMEM(factors.shape, F32),
            pltpu.VMEM((SETS, 64, columns), F32),
            pltpu.VMEM((SETS, 64, 512), F32),
            pltpu.VMEM((SETS - 1, 3, 16, 512), F32),
            pltpu.VMEM((SETS - 1, 16, 512), F32),
            pltpu.VMEM((SETS - 1, 7, 8, 128), F32),
            pltpu.VMEM((2, len(STEPS), 8, 128), F32),
            pltpu.VMEM((groups, group, columns), F32),
            pltpu.VMEM((depth, columns), F32),
            pltpu.VMEM((depth, columns), BF16),
            pltpu.VMEM((depth, columns), BF16),
            pltpu.VMEM((32, 128), F32),
            pltpu.VMEM((16, 128), F32),
            pltpu.VMEM((4, 16, 128), F32),
            pltpu.VMEM((8, 16, 128), F32),
            pltpu.VMEM((4, 32, 128), F32),
            dma((CHUNKS,)), dma((2,)), dma((10,)), dma((3, 2)), dma((3, 2)),
            dma((SETS + 1,)), dma((SETS + 1,)),
            dma((SETS + 1, 3)), dma((SETS + 1, 3)),
            dma((SETS + 1, 7)), dma((SETS + 1, 7)),
            dma((SETS, 7)), dma((SETS, 7)),
            dma((SETS + 1, 3)), dma((SETS + 1, 3)),
            dma((SETS + 1, 2)), dma((SETS + 1, 2)),
            dma((2, len(STEPS))), dma((2, len(STEPS))),
            dma((2, len(STEPS))), dma((2, len(STEPS))),
            pltpu.SemaphoreType.REGULAR((4,)),
        ],
        compiler_params=pltpu.CompilerParams(
            collective_id=0, has_side_effects=True, vmem_limit_bytes=40 * 2**20
        ),
        name="gather_and_reduce",
    )(*(pltpu.with_memory_space_constraint(operand, pltpu.HBM) for operand in (eigvecs, own, factors)))

    operands = (eigvecs, vh, vl, ch, cl)
    return pl.pallas_call(
        update_kernel,
        out_shape=jax.ShapeDtypeStruct((rows, columns), F32),
        in_specs=[pl.BlockSpec(memory_space=pltpu.VMEM)] * len(operands),
        out_specs=any_space,
        scratch_shapes=[pltpu.VMEM((rows, columns), F32), dma((PIECES,))],
        compiler_params=pltpu.CompilerParams(vmem_limit_bytes=16 * 2**20),
        name="update",
    )(*(pltpu.with_memory_space_constraint(operand, pltpu.VMEM) for operand in operands))


def solution(mesh):
    placed = (P("row", "col"), P(None, "row", "col"), P())
    return jax.shard_map(
        body, mesh=mesh, in_specs=placed, out_specs=P("row", "col"), check_vma=False
    )
```

```python
import jax
import jax.numpy as jnp
from jax import lax
from jax.experimental import pallas as pl
from jax.experimental.pallas import tpu as pltpu
from jax.sharding import PartitionSpec as P

MESH = pl.DeviceIdType.MESH
F32, BF16 = jnp.float32, jnp.bfloat16
BLOCKS = 2
Y_SIZE = 4
CHUNKS = 6
PIECES = 12

SET_GROUPS = ((0, 1), (6, 3), (7, 2), (4, 5))
SETS = len(SET_GROUPS)
STEPS = sorted(
    ((dz, dx) for dz in range(8) for dx in range(4) if dz or dx),
    key=lambda step: -min(step[0], 8 - step[0]) - min(step[1], 4 - step[1]),
)


def line(g):
    return g % 2 * 128 + g // 2 * 32


def split(value):
    high = value.astype(BF16)
    return high, (value - high.astype(F32)).astype(BF16)


def dot(left, right, dims):
    return lax.dot_general(left, right, (dims, ((), ())), preferred_element_type=F32)


def product(left, right, dims=((1,), (0,))):
    (lh, ll), (rh, rl) = left, right
    return dot(lh, rh, dims) + (dot(lh, rl, dims) + dot(ll, rh, dims))


def reduce_kernel(
    x_hbm, v_hbm, f_hbm, vh_out, vl_out, ch_out, cl_out,
    x_buf, xh, xl, v_all, vh_all, vl_all, vh_t, vl_t, f_ref, tri, s_loc, core_in, x_in, x_sum, z_in, d_in, s_sum, c_part, ch, cl,
    g_loc, g_core, g_xin, g_zin, g_sum,
    x_sem, v_sem, out_sem, vs_sem, vr_sem,
    c_s, c_r, xs_s, xs_r, zs_s, zs_r, zg_s, zg_r, xg_s, xg_r, cg_s, cg_r, ds_s, ds_r, dg_s, dg_r, greeted,
):
    row, y = lax.axis_index("row"), lax.axis_index("col")
    z, x, core = row // 8, (row // 2) % 4, row % 2
    rows = x_hbm.shape[0] // CHUNKS

    def at(z_, x_, core_, y_):
        return ((z_ * 4 + x_) * 2 + core_, y_)

    other = at(z, x, 1 - core, y)
    x_peer = [at(z, (x + d) % 4, core, y) for d in range(1, 4)]
    z_peer = [at((z + d) % 8, x, core, y) for d in range(1, 8)]
    plane = [at((z + dz) % 8, (x + dx) % 4, core, y) for dz, dx in STEPS]
    y_peer = [at(z, x, core, (y + d) % 4) for d in range(1, 4)]
    up, down = y_peer[0], y_peer[2]
    mine = pl.ds(pl.multiple_of(core * 512, 512), 512)
    theirs = pl.ds(pl.multiple_of((1 - core) * 512, 512), 512)

    z_near = [at((z + d) % 8, x, core, y) for d in (1, 7)]
    z_next = [at((z + d) % 8, x, core, y) for d in (2, 6)]
    x_near = [x_peer[0], x_peer[2]]

    def greet(semaphore, devices):
        for device in devices:
            pl.semaphore_signal(semaphore, inc=1, device_id=device, device_id_type=MESH)

    barrier = pltpu.get_barrier_semaphore()
    greet(barrier, [up, down, other] + x_near + z_near)

    own = pltpu.make_async_copy(v_hbm, v_all.at[0:2], v_sem.at[0])
    own.start()
    factors = pltpu.make_async_copy(f_hbm, f_ref, v_sem.at[1])
    factors.start()

    def take(i):
        x_copies[i].wait()

        @pl.loop(0, rows // 64)
        def _(j):
            part = pl.ds(pl.multiple_of(i * rows + j * 64, 64), 64)
            high, low = split(x_buf[part, :])
            xh[part, :] = high
            xl[part, :] = low

    own.wait()
    pl.semaphore_wait(barrier, 7)
    pending = []

    def send(src, dst, s_sem, r_sem, device):
        copy = pltpu.make_async_remote_copy(
            src_ref=src, dst_ref=dst, send_sem=s_sem, recv_sem=r_sem, device_id=device, device_id_type=MESH
        )
        copy.start()
        pending.append(copy)
        return copy

    from_down, from_up, opposite = [None, None], [None, None], [None, None]
    for i in range(2):
        from_down[i] = send(v_all.at[i], v_all.at[6 + i], vs_sem.at[0, i], vr_sem.at[0, i], up)
        b = 1 - i
        from_up[b] = send(v_all.at[b], v_all.at[2 + b], vs_sem.at[1, b], vr_sem.at[1, b], down)

    x_copies = []
    for i in range(CHUNKS):
        part = pl.ds(i * rows, rows)
        copy = pltpu.make_async_copy(x_hbm.at[part], x_buf.at[part], x_sem.at[i])
        copy.start()
        x_copies.append(copy)
    greet(greeted.at[0], z_near)
    greet(greeted.at[1], x_near)
    for i in range(CHUNKS):
        take(i)
        if i == 2:
            pl.semaphore_wait(greeted.at[0], 2)
            greet(greeted.at[2], z_next)

    core_copies, x_sends, z_sends, z_shares, x_shares, core_shares = ([[] for _ in range(SETS + 1)] for _ in range(6))

    def arrived(copies):
        while copies:
            copies.pop(0).wait_recv()

    def flush(left=0):
        while len(pending) > left:
            pending.pop(0).wait_send()

    def partial(i):
        groups = SET_GROUPS[i]
        vh, vl = split(jnp.concatenate([v_all[g] for g in groups], axis=0))
        both = jnp.concatenate([vh, vl], axis=0)

        def columns(part):
            first = dot(both, xh[:, part], ((1,), (0,)))
            second = dot(vh, xl[:, part], ((1,), (0,)))
            s_loc[i, :, part] = first[:64] + (first[64:] + second)

        columns(theirs)
        core_copies[i].append(send(s_loc.at[i, :, theirs], core_in.at[i], c_s.at[i], c_r.at[i], other))
        columns(mine)
        for n, g in enumerate(groups):
            spot = slice(line(g), line(g) + 32)
            vh_all[spot] = vh[32 * n : 32 * n + 32]
            vl_all[spot] = vl[32 * n : 32 * n + 32]

    def add_core(i):
        arrived(core_copies[i])
        s_loc[i, :, mine] = s_loc[i, :, mine] + core_in[i]

    def group(i, half):
        first, second = SET_GROUPS[i]
        return first + half * (second - first)

    def x_rows(x_):
        return pl.ds(pl.multiple_of(x_ * 16, 16), 16)

    def z_tile(z_):
        return pl.ds(pl.multiple_of(z_ // 4 * 8, 8), 8), pl.multiple_of(z_ % 4 * 128, 128)

    def to_x(i):
        add_core(i)
        for d in range(1, 4):
            x_sends[i].append(
                send(
                    s_loc.at[i, x_rows((x + d) % 4), mine], x_in.at[i, d - 1],
                    xs_s.at[i, d - 1], xs_r.at[i, d - 1], x_peer[d - 1],
                )
            )

    def to_z(i):
        arrived(x_sends[i])
        x_sum[i] = (s_loc[i, x_rows(x), mine] + x_in[i, 0]) + (x_in[i, 1] + x_in[i, 2])
        for d in range(1, 8):
            r, c = z_tile((z + d) % 8)
            z_sends[i].append(
                send(
                    x_sum.at[i, r, pl.ds(c, 128)], z_in.at[i, d - 1],
                    zs_s.at[i, d - 1], zs_r.at[i, d - 1], z_peer[d - 1],
                )
            )

    def share_z(i):
        arrived(z_sends[i])
        r, c = z_tile(z)
        total = x_sum[i, r, pl.ds(c, 128)]
        for d in range(7):
            total = total + z_in[i, d]
        first = pl.multiple_of(x % 2 * 16 + z // 4 * 8, 8)
        spot = s_sum.at[group(i, x // 2), pl.ds(first, 8), pl.ds(pl.multiple_of(core * 512 + c, 128), 128)]
        spot[...] = total
        for d in range(1, 8):
            z_shares[i].append(send(spot, spot, zg_s.at[i, d - 1], zg_r.at[i, d - 1], z_peer[d - 1]))

    def share_x(i):
        arrived(z_shares[i])
        spot = s_sum.at[group(i, x // 2), pl.ds(pl.multiple_of(x % 2 * 16, 16), 16), mine]
        for d in range(1, 4):
            x_shares[i].append(send(spot, spot, xg_s.at[i, d - 1], xg_r.at[i, d - 1], x_peer[d - 1]))

    def tile(z_, x_):
        return pl.ds(pl.multiple_of(z_ * 8, 8), 8), pl.ds(pl.multiple_of(core * 512 + x_ * 128, 128), 128)

    def to_plane(i):
        add_core(i)
        for k, (dz, dx) in enumerate(STEPS):
            r, c = tile((z + dz) % 8, (x + dx) % 4)
            x_sends[i].append(
                send(s_loc.at[i, r, c], d_in.at[i - 2, k], ds_s.at[i - 2, k], ds_r.at[i - 2, k], plane[k])
            )

    def share_plane(i):
        arrived(x_sends[i])
        r, c = tile(z, x)
        total = s_loc[i, r, c]
        for k in range(len(STEPS)):
            total = total + d_in[i - 2, k]
        spot = s_sum.at[group(i, z // 4), pl.ds(pl.multiple_of(z % 4 * 8, 8), 8), c]
        spot[...] = total
        for k in range(len(STEPS)):
            x_shares[i].append(send(spot, spot, dg_s.at[i - 2, k], dg_r.at[i - 2, k], plane[k]))

    def share_core(i):
        arrived(x_shares[i])
        for k, g in enumerate(SET_GROUPS[i]):
            spot = s_sum.at[g, :, mine]
            core_shares[i].append(send(spot, spot, cg_s.at[i, k], cg_r.at[i, k], other))

    PAIRS = ((0, 0), (0, 3), (1, 3), (3, 0))
    g_half = pl.ds(pl.multiple_of(core * 16, 16), 16)
    g_other = pl.ds(pl.multiple_of((1 - core) * 16, 16), 16)

    def g_partial():
        second, first = (
            tuple(jnp.concatenate([v[line(g) : line(g) + 32] for g in groups], axis=0) for v in (vh_all, vl_all))
            for groups in ((1, 3, 7), (0, 6))
        )
        pairs = product(second, first, ((1,), (1,)))
        place = {0: 0, 1: 1, 3: 2}, {0: 0, 3: 1}
        g_loc[...] = jnp.concatenate(
            [
                pairs[32 * place[0][i] : 32 * place[0][i] + 32, 32 * place[1][j] : 32 * place[1][j] + 32]
                for i, j in PAIRS
            ],
            axis=1,
        )
        core_copies[SETS].append(send(g_loc.at[g_other], g_core, c_s.at[SETS], c_r.at[SETS], other))

    def g_to_x():
        arrived(core_copies[SETS])
        g_xin[x] = g_loc[g_half, :] + g_core[...]
        for d in range(1, 4):
            x_sends[SETS].append(
                send(g_xin.at[x], g_xin.at[x], xs_s.at[SETS, d - 1], xs_r.at[SETS, d - 1], x_peer[d - 1])
            )

    def g_to_z():
        arrived(x_sends[SETS])
        g_zin[z] = (g_xin[0] + g_xin[1]) + (g_xin[2] + g_xin[3])
        for d in range(1, 8):
            z_sends[SETS].append(
                send(g_zin.at[z], g_zin.at[z], zs_s.at[SETS, d - 1], zs_r.at[SETS, d - 1], z_peer[d - 1])
            )

    def g_share_core():
        arrived(z_sends[SETS])
        total = g_zin[0]
        for d in range(1, 8):
            total = total + g_zin[d]
        spot = g_sum.at[0, g_half]
        spot[...] = total
        core_shares[SETS].append(send(spot, spot, cg_s.at[SETS, 0], cg_r.at[SETS, 0], other))

    def g_share_y():
        arrived(core_shares[SETS])
        for d in range(1, 4):
            x_shares[SETS].append(
                send(g_sum.at[0], g_sum.at[4 - d], xg_s.at[SETS, d - 1], xg_r.at[SETS, d - 1], y_peer[d - 1])
            )

    def g_whole():
        arrived(x_shares[SETS])
        lines = []
        for i in range(4):
            blocks = []
            for j in range(4):
                d = (i - j) % 4
                source = (i, i, i + 3, i + 1)[d] % 4
                blocks.append(g_sum[source, :, 32 * d : 32 * d + 32])
            lines.append(jnp.concatenate(blocks, axis=1))
        return jnp.concatenate(lines, axis=0)

    outs = []

    def leave(src, dst):
        copy = pltpu.make_async_copy(src, dst, out_sem.at[len(outs)])
        copy.start()
        outs.append(copy)

    partial(0)
    pl.semaphore_wait(greeted.at[1], 2)
    to_x(0)
    pl.semaphore_wait(greeted.at[2], 2)
    greet(greeted.at[3], z_peer)

    from_down[0].wait_recv()
    from_up[1].wait_recv()
    partial(1)
    opposite[0] = send(v_all.at[6], v_all.at[4], vs_sem.at[2, 0], vr_sem.at[2, 0], up)
    opposite[1] = send(v_all.at[3], v_all.at[5], vs_sem.at[2, 1], vr_sem.at[2, 1], down)
    to_x(1)

    factors.wait()
    upper = lax.broadcasted_iota(jnp.int32, (128, 128), 0) <= lax.broadcasted_iota(jnp.int32, (128, 128), 1)
    turn = (Y_SIZE - y) % Y_SIZE * 32
    for b in range(2):
        tri[b] = pltpu.roll(pltpu.roll(jnp.where(upper, f_ref[b], 0.0), turn, 0), turn, 1)

    from_down[1].wait_recv()
    from_up[0].wait_recv()
    partial(2)
    to_z(0)
    g_partial()
    pl.semaphore_wait(greeted.at[3], 7)
    to_plane(2)
    g_to_x()
    to_z(1)
    opposite[0].wait_recv()
    opposite[1].wait_recv()
    partial(3)
    to_plane(3)
    share_z(0)
    g_to_z()
    share_z(1)
    share_plane(2)
    share_x(0)

    @pl.loop(0, CHUNKS)
    def _(i):
        part = pl.ds(pl.multiple_of(i * rows, rows), rows)
        vh_t[part, :] = vh_all[:, part].T
        vl_t[part, :] = vl_all[:, part].T

    flush(40)
    leave(vh_t, vh_out)
    leave(vl_t, vl_out)

    share_plane(3)
    g_share_core()
    share_x(1)
    g_share_y()
    share_core(0)
    share_core(2)

    t0, t1 = split(tri[0]), split(tri[1])
    mixed = product(split(product(t1, split(g_whole()))), t0)
    matrix = split(
        jnp.concatenate(
            [
                jnp.concatenate([tri[0], jnp.zeros((128, 128), F32)], axis=1),
                jnp.concatenate([-mixed, tri[1]], axis=1),
            ],
            axis=0,
        )
    )

    def part_of(i):
        high, low = matrix
        return jnp.concatenate([m[:, line(g) : line(g) + 32] for m in (high, high, low) for g in SET_GROUPS[i]], axis=1)

    def term(i, wide, cols):
        sh, sl = split(jnp.concatenate([s_sum[g, :, cols] for g in SET_GROUPS[i]], axis=0))
        return dot(wide, jnp.concatenate([sh, sl, sh], axis=0), ((1,), (0,)))

    def add_set(i, first=False):
        arrived(core_shares[i])
        wide = part_of(i)
        for j in range(4):
            cols = pl.ds(j * 256, 256)
            c_part[:, cols] = term(i, wide, cols) if first else c_part[:, cols] + term(i, wide, cols)

    def finish(start, wide):
        for j in range(2):
            cols = pl.ds(pl.multiple_of(start + j * 256, 256), 256)
            ch[:, cols], cl[:, cols] = split(c_part[:, cols] + term(3, wide, cols))
            leave(ch.at[:, cols], ch_out.at[:, cols])
            leave(cl.at[:, cols], cl_out.at[:, cols])

    add_set(0, first=True)
    share_core(1)
    flush(40)
    add_set(2)
    share_core(3)
    add_set(1)
    wide = part_of(3)
    finish(core * 512, wide)
    arrived(core_shares[3])
    finish((1 - core) * 512, wide)

    for copy in outs:
        copy.wait()
    flush()


def update_kernel(x_ref, vh_ref, vl_ref, ch_ref, cl_ref, out, buffer, sem):
    step = x_ref.shape[0] // PIECES
    copies = []
    for i in range(PIECES):
        part = pl.ds(i * step, step)
        for j in range(4):
            cols = pl.ds(j * 256, 256)
            change = product((vh_ref[part, :], vl_ref[part, :]), (ch_ref[:, cols], cl_ref[:, cols]))
            buffer[part, cols] = x_ref[part, cols] - change
        copy = pltpu.make_async_copy(buffer.at[part], out.at[part], sem.at[i])
        copy.start()
        copies.append(copy)
    for copy in copies:
        copy.wait()


def body(eigvecs, reflectors, factors):
    rows, columns = eigvecs.shape
    own = reflectors.transpose(0, 2, 1)
    group = own.shape[1]
    dma = pltpu.SemaphoreType.DMA
    any_space = pl.BlockSpec(memory_space=pl.ANY)
    groups = Y_SIZE * BLOCKS
    depth = groups * group
    vh, vl, ch, cl = pl.pallas_call(
        reduce_kernel,
        out_shape=[
            jax.ShapeDtypeStruct((rows, depth), BF16),
            jax.ShapeDtypeStruct((rows, depth), BF16),
            jax.ShapeDtypeStruct((depth, columns), BF16),
            jax.ShapeDtypeStruct((depth, columns), BF16),
        ],
        in_specs=[any_space, any_space, any_space],
        out_specs=[any_space, any_space, any_space, any_space],
        scratch_shapes=[
            pltpu.VMEM((rows, columns), F32),
            pltpu.VMEM((rows, columns), BF16),
            pltpu.VMEM((rows, columns), BF16),
            pltpu.VMEM((groups, group, rows), F32),
            pltpu.VMEM((depth, rows), BF16),
            pltpu.VMEM((depth, rows), BF16),
            pltpu.VMEM((rows, depth), BF16),
            pltpu.VMEM((rows, depth), BF16),
            pltpu.VMEM(factors.shape, F32),
            pltpu.VMEM(factors.shape, F32),
            pltpu.VMEM((SETS, 64, columns), F32),
            pltpu.VMEM((SETS, 64, 512), F32),
            pltpu.VMEM((SETS - 1, 3, 16, 512), F32),
            pltpu.VMEM((SETS - 1, 16, 512), F32),
            pltpu.VMEM((SETS - 1, 7, 8, 128), F32),
            pltpu.VMEM((2, len(STEPS), 8, 128), F32),
            pltpu.VMEM((groups, group, columns), F32),
            pltpu.VMEM((depth, columns), F32),
            pltpu.VMEM((depth, columns), BF16),
            pltpu.VMEM((depth, columns), BF16),
            pltpu.VMEM((32, 128), F32),
            pltpu.VMEM((16, 128), F32),
            pltpu.VMEM((4, 16, 128), F32),
            pltpu.VMEM((8, 16, 128), F32),
            pltpu.VMEM((4, 32, 128), F32),
            dma((CHUNKS,)), dma((2,)), dma((10,)), dma((3, 2)), dma((3, 2)),
            dma((SETS + 1,)), dma((SETS + 1,)),
            dma((SETS + 1, 3)), dma((SETS + 1, 3)),
            dma((SETS + 1, 7)), dma((SETS + 1, 7)),
            dma((SETS, 7)), dma((SETS, 7)),
            dma((SETS + 1, 3)), dma((SETS + 1, 3)),
            dma((SETS + 1, 2)), dma((SETS + 1, 2)),
            dma((2, len(STEPS))), dma((2, len(STEPS))),
            dma((2, len(STEPS))), dma((2, len(STEPS))),
            pltpu.SemaphoreType.REGULAR((4,)),
        ],
        compiler_params=pltpu.CompilerParams(
            collective_id=0, has_side_effects=True, vmem_limit_bytes=40 * 2**20
        ),
        name="gather_and_reduce",
    )(*(pltpu.with_memory_space_constraint(operand, pltpu.HBM) for operand in (eigvecs, own, factors)))

    operands = (eigvecs, vh, vl, ch, cl)
    return pl.pallas_call(
        update_kernel,
        out_shape=jax.ShapeDtypeStruct((rows, columns), F32),
        in_specs=[pl.BlockSpec(memory_space=pltpu.VMEM)] * len(operands),
        out_specs=any_space,
        scratch_shapes=[pltpu.VMEM((rows, columns), F32), dma((PIECES,))],
        compiler_params=pltpu.CompilerParams(vmem_limit_bytes=16 * 2**20),
        name="update",
    )(*(pltpu.with_memory_space_constraint(operand, pltpu.VMEM) for operand in operands))


def solution(mesh):
    placed = (P("row", "col"), P(None, "row", "col"), P())
    return jax.shard_map(
        body, mesh=mesh, in_specs=placed, out_specs=P("row", "col"), check_vma=False
    )
```
